512 devices in a mesh: fsdp: 32 (over z, x), tensor: 16 (over y, core).
Axes of the slice: x: 4, y: 8, z: 8, core: 2. Of those that a mesh axis runs over, the one named last changes fastest.
Arguments:
- gate_pre: bfloat16 [4096, 26624], P('fsdp', 'tensor'), may hold values from -6 to 6
- up_pre: bfloat16 [4096, 26624], P('fsdp', 'tensor'), may hold values from -6 to 6
- out_grad: bfloat16 [4096, 8192], P('fsdp', 'tensor'), may hold values from -6 to 6
- down_blocks: bfloat16 [96, 16, 128, 128], P('fsdp', 'tensor'), may hold values from -0.109375 to 0.109375
- block_rows: int32 [96, 16], P(None, 'tensor'), may hold values from 0 to 12, as said below
- block_cols: int32 [96, 16], P(None, 'tensor'), may hold values from 0 to 63
Outputs:
- output: bfloat16 [4096, 8192], P('fsdp', 'tensor')
- d_gate: bfloat16 [4096, 26624], P('fsdp', 'tensor')
- d_up: bfloat16 [4096, 26624], P('fsdp', 'tensor')
- grad_blocks: float32 [96, 16, 128, 128], P('fsdp', 'tensor')
The draws below stay inside these ranges and needn't reach their ends.
Inputs may be any that keep to these rules, and one draw needn't show every extreme that they name: Within one rank t the pairs (block_rows[k, t], block_cols[k, t]) are distinct.
All inputs are finite; a program needn't handle non-finite values.
Results may differ from the reference program's by a relative error of at most 0.02.
Values may be sent and summed in bfloat16 or wider, within the bound.
No kernel may reach another device: no remote copies, remote signals or barrier semaphores. Data moves between devices by JAX's collectives and lax.ppermute only.
A program may use at most 64 MiB of HBM per device.

```python
import jax
import jax.numpy as jnp
from jax import lax

BLK = 128
D = 8192
HID_TILES = 13
GROUP_BLOCKS = 96
TOK_DEV = 128
WIDTH_TILES = 64
FF = 26624
RANKS = 16
TOKENS = 4096
N_FSDP = 32


def block_positions(key):
    rank_keys = jax.random.split(key, RANKS)
    shuffled = jax.vmap(lambda single: jax.random.permutation(single, HID_TILES * WIDTH_TILES))(rank_keys)
    return shuffled[:, :GROUP_BLOCKS].T.astype(jnp.int32)


def draw_block_rows(key, part):
    places = block_positions(key)
    return (places // WIDTH_TILES).astype(jnp.int32)


def draw_block_cols(key, part):
    places = block_positions(key)
    return (places % WIDTH_TILES).astype(jnp.int32)


def levels(key, extent, cuts, least, high):
    factor_of = 1.0
    for position, parts in cuts:
        steps = jax.random.uniform(jax.random.fold_in(jax.random.fold_in(key, 6), position), (parts,), jnp.float32, least / len(cuts), high / len(cuts))
        factor_of = factor_of * jnp.repeat(jnp.exp(steps), extent[position] // parts).reshape((-1,) + (1,) * (len(extent) - 1 - position))
    return factor_of


def bell_draw(rng, extent, deviation, reach, cuts=(), kind=jnp.bfloat16):
    values = jax.random.normal(rng, extent, jnp.float32) * deviation
    if len(cuts) > 0:
        values = levels(rng, extent, cuts, -0.22, 0.18) * values
    return jnp.clip(values, min=-reach, max=reach).astype(kind)


def setup_inputs(seed: int = 0) -> dict:
    key_list = jax.random.split(jax.random.key(seed), 7)
    gate_pre = bell_draw(key_list[0], (TOKENS, FF), 1.0, 6.0, ((0, 32), (1, 16)))
    up_pre = bell_draw(key_list[1], (TOKENS, FF), 1.0, 6.0, ((0, 32), (1, 16)))
    out_grad = bell_draw(key_list[2], (TOKENS, D), 1.0, 6.0, ((0, 32), (1, 16)))
    down_blocks = bell_draw(key_list[3], (GROUP_BLOCKS, RANKS, BLK, BLK), (GROUP_BLOCKS * RANKS * BLK // WIDTH_TILES) ** -0.5, 0.109375, ((0, 32), (1, 16)))
    block_rows = draw_block_rows(jax.random.fold_in(key_list[6], 71), 0)
    block_cols = draw_block_cols(jax.random.fold_in(key_list[6], 71), 0)
    return {"gate_pre": gate_pre, "up_pre": up_pre, "out_grad": out_grad, "down_blocks": down_blocks, "block_rows": block_rows, "block_cols": block_cols}


def reference(gate_pre, up_pre, out_grad, down_blocks, block_rows, block_cols):
    gate_full = gate_pre.astype(jnp.float32)
    up_full = up_pre.astype(jnp.float32)
    sigma = jax.nn.sigmoid(gate_full)
    hidden = (gate_full * sigma * up_full).astype(jnp.bfloat16)
    span = HID_TILES * BLK
    hidden_ranks = hidden.reshape(TOKENS, RANKS, span).transpose(1, 0, 2)
    blocks_ranks = down_blocks.transpose(1, 0, 2, 3)
    rows_ranks = block_rows.T
    columns_ranks = block_cols.T
    grad_tiles = out_grad.astype(jnp.float32).reshape(TOKENS, WIDTH_TILES, BLK)

    def per_rank(summed, packed):
        hidden_rank, blocks, tile_rows, tile_columns = packed
        hidden_tiles = hidden_rank.astype(jnp.float32).reshape(TOKENS, HID_TILES, BLK)
        weights = blocks.astype(jnp.float32)
        chosen = jnp.take(hidden_tiles, tile_rows, axis=1)
        contrib = jnp.einsum("tbi,bij->tbj", chosen, weights)
        partial_out = jnp.zeros((TOKENS, WIDTH_TILES, BLK), jnp.float32).at[:, tile_columns].add(contrib)
        partial_out = partial_out.astype(jnp.bfloat16).reshape(TOKENS, D)
        summed = summed + partial_out.astype(jnp.float32)
        grad_chosen = jnp.take(grad_tiles, tile_columns, axis=1)
        backed = jnp.einsum("tbj,bij->tbi", grad_chosen, weights)
        grad_hidden = jnp.zeros((TOKENS, HID_TILES, BLK), jnp.float32).at[:, tile_rows].add(backed)
        terms = jnp.einsum("ftbi,ftbj->fbij",
                           chosen.reshape(N_FSDP, TOK_DEV, GROUP_BLOCKS, BLK),
                           grad_chosen.reshape(N_FSDP, TOK_DEV, GROUP_BLOCKS, BLK)).astype(jnp.bfloat16)
        grads = jnp.sum(terms.astype(jnp.float32), axis=0)
        return summed, (grad_hidden.reshape(TOKENS, span), grads)

    start_sum = jnp.zeros((TOKENS, D), jnp.float32)
    summed, (hidden_grads, grads_all) = lax.scan(
        per_rank, start_sum, (hidden_ranks, blocks_ranks, rows_ranks, columns_ranks))
    output = summed.astype(jnp.bfloat16)
    grad_hidden = hidden_grads.transpose(1, 0, 2).reshape(TOKENS, FF)
    d_gate = (grad_hidden * up_full * sigma * (1.0 + gate_full * (1.0 - sigma))).astype(jnp.bfloat16)
    d_up = (grad_hidden * gate_full * sigma).astype(jnp.bfloat16)
    grad_blocks = grads_all.transpose(1, 0, 2, 3)
    return (output, d_gate, d_up, grad_blocks)
```

```python
import functools

import jax
import jax.numpy as jnp
from jax import lax
from jax.experimental import pallas as pl
from jax.experimental.pallas import tpu as pltpu
from jax.sharding import PartitionSpec as P

BLK = 128
HID_TILES = 13
WIDTH_TILES = 64
GROUP_BLOCKS = 96
OWNED = 3
FAR = 2
NX, NY, NZ = 4, 8, 8
STEP = 8
VMEM_BYTES = 48 * 1024 * 1024

SMEM = pl.BlockSpec(memory_space=pltpu.SMEM)
VMEM = pl.BlockSpec(memory_space=pltpu.VMEM)


def x_shift(step):
    return [(z * NX + x, z * NX + (x + step) % NX) for z in range(NZ) for x in range(NX)]


CORE_SWAP = [(t, t ^ 1) for t in range(2 * NY)]
Z_GROUPS = [[z * NX + x for z in range(NZ)] for x in range(NX)]
Y_GROUPS = [[y * 2 + c for y in range(NY)] for c in range(2)]


def call(kernel, outs, ins, scratch=(), flops=0, moved=0):
    return pl.pallas_call(
        kernel,
        out_shape=outs,
        in_specs=[SMEM if a.dtype == jnp.int32 else VMEM for a in ins],
        out_specs=jax.tree.map(lambda _: VMEM, outs),
        scratch_shapes=list(scratch),
        compiler_params=pltpu.CompilerParams(vmem_limit_bytes=VMEM_BYTES),
        cost_estimate=pl.CostEstimate(flops=flops, bytes_accessed=moved, transcendentals=0),
    )(*ins)


def tiles(n, dtype=jnp.bfloat16):
    return jax.ShapeDtypeStruct((n, BLK, BLK), dtype)


def block_of(z, x, place):
    return (z * NX + x) * OWNED + place


def far_at(a, i, me_x, sign):
    return block_of(i // FAR, lax.rem(me_x + sign * a + NX, NX), lax.rem(i, FAR))


def near_at(i, me_x, sign):
    return block_of(i // NX, lax.rem(me_x + sign * lax.rem(i, NX) + NX, NX), FAR)


def each_block(parts, me_x, sign, visit):
    for a, ref in enumerate(parts):
        def some(g, carry, a=a, ref=ref):
            entries = [g * STEP + j for j in range(STEP)]
            visit(ref, [(i, far_at(a, i, me_x, sign) if a < NX else near_at(i, me_x, sign)) for i in entries])
            return carry
        lax.fori_loop(0, ref.shape[0] // STEP, some, 0)


def hidden_kernel(gate_ref, up_ref, hid_ref, hid_t_ref):
    for r in range(HID_TILES):
        here = slice(r * BLK, (r + 1) * BLK)
        gate = gate_ref[:, here].astype(jnp.float32)
        hidden = gate * jax.nn.sigmoid(gate) * up_ref[:, here].astype(jnp.float32)
        hid_ref[r] = hidden.astype(jnp.bfloat16)
        hid_t_ref[r] = hidden.T.astype(jnp.bfloat16)


def terms_kernel(rows_ref, cols_ref, me_ref, hid_t_ref, grad_ref, *out_refs):
    def visit(ref, entries):
        for i, k in entries:
            ref[i] = jnp.dot(
                hid_t_ref[rows_ref[k]], grad_ref[cols_ref[k]], preferred_element_type=jnp.float32
            ).astype(jnp.bfloat16)
    each_block(out_refs, me_ref[0], 1, visit)


def forward_kernel(rows_ref, cols_ref, me_ref, hid_ref, *refs):
    parts, (out_ref, total) = refs[:NX + 1], refs[NX + 1:]
    total[...] = jnp.zeros_like(total)

    def visit(ref, entries):
        found = [
            (cols_ref[k], jnp.dot(hid_ref[rows_ref[k]], ref[i], preferred_element_type=jnp.float32)) for i, k in entries
        ]
        for c, value in found:
            total[c] += value
    each_block(parts, me_ref[0], -1, visit)

    def put(y, carry):
        for j in range(8):
            out_ref[y * 8 + j] = total[y * 8 + j].astype(jnp.bfloat16)
        return carry
    lax.fori_loop(0, NY, put, 0)


def backward_kernel(rows_ref, cols_ref, me_ref, grad_ref, gate_ref, up_ref, *refs):
    parts, (d_gate_ref, d_up_ref, total) = refs[:NX + 1], refs[NX + 1:]
    total[...] = jnp.zeros_like(total)

    def visit(ref, entries):
        found = [
            (rows_ref[k], lax.dot_general(
                grad_ref[cols_ref[k]], ref[i], (((1,), (1,)), ((), ())), preferred_element_type=jnp.float32
            )) for i, k in entries
        ]
        for r, value in found:
            total[r] += value
    each_block(parts, me_ref[0], -1, visit)
    for r in range(HID_TILES):
        here = slice(r * BLK, (r + 1) * BLK)
        gate = gate_ref[:, here].astype(jnp.float32)
        up = up_ref[:, here].astype(jnp.float32)
        sigma = jax.nn.sigmoid(gate)
        back = total[r]
        d_gate_ref[:, here] = (back * up * sigma * (1.0 + gate * (1.0 - sigma))).astype(jnp.bfloat16)
        d_up_ref[:, here] = (back * gate * sigma).astype(jnp.bfloat16)


def near_sum_kernel(arrived_ref, *out_refs):
    for b, out_ref in enumerate(out_refs):
        total = arrived_ref[b].astype(jnp.float32)
        for z in range(1, NZ):
            total += arrived_ref[z * NX + b].astype(jnp.float32)
        out_ref[0] = total.astype(jnp.bfloat16)


def block_sum_kernel(far_ref, *refs):
    near_refs, out_ref = refs[:NX], refs[NX]
    for j in range(FAR):
        total = far_ref[j].astype(jnp.float32)
        for z in range(1, NZ):
            total += far_ref[z * FAR + j].astype(jnp.float32)
        out_ref[j] = total
    total = near_refs[0][0].astype(jnp.float32)
    for ref in near_refs[1:]:
        total += ref[0].astype(jnp.float32)
    out_ref[FAR] = total


def z_exchange(a):
    return lax.all_to_all(a, "fsdp", 0, 0, tiled=True, axis_index_groups=Z_GROUPS)


def to_all(a):
    return jnp.broadcast_to(a[None], (NZ, *a.shape)).reshape(NZ * a.shape[0], BLK, BLK)


def shards(gate_pre, up_pre, out_grad, down_blocks, block_rows, block_cols):
    rows, cols = block_rows[:, 0], block_cols[:, 0]
    me = jnp.stack([lax.rem(lax.axis_index("fsdp"), NX), lax.rem(lax.axis_index("tensor"), 2)]).astype(jnp.int32)
    macs = GROUP_BLOCKS * BLK**3
    blocks = down_blocks.reshape(OWNED, BLK, BLK)

    with jax.named_scope("gather_out_grad"):
        grad_tiles = out_grad.reshape(BLK, 4, BLK).transpose(1, 0, 2)
        grad_tiles, blocks = lax.optimization_barrier((grad_tiles, blocks))
        grad_tiles = lax.all_gather(grad_tiles, "tensor", axis=0, tiled=True)
    with jax.named_scope("gather_blocks"):
        far = z_exchange(to_all(blocks[:FAR]))
        near = blocks[FAR:]
        near = jnp.concatenate([near] + [lax.ppermute(near, "fsdp", x_shift(s)) for s in range(1, NX)], axis=0)
        near = z_exchange(to_all(near))
        parts = [far] + [lax.ppermute(far, "fsdp", x_shift(s)) for s in range(1, NX)] + [near]
    with jax.named_scope("hidden"):
        hid, hid_t = call(hidden_kernel, (tiles(HID_TILES), tiles(HID_TILES)), (gate_pre, up_pre), flops=10**9, moved=4 * 10**6)
    with jax.named_scope("terms"):
        outs = tuple(tiles(NZ * FAR) for _ in range(NX)) + (tiles(NZ * NX),)
        terms = call(terms_kernel, outs, (rows, cols, me, hid_t, grad_tiles), flops=8 * macs, moved=6 * 10**6)
        terms, hid = lax.optimization_barrier((terms, hid))
    with jax.named_scope("sum_terms_first"):
        far_terms = [terms[0]] + [lax.ppermute(terms[s], "fsdp", x_shift(s)) for s in range(1, NX)]
        near_terms = z_exchange(terms[NX])
    with jax.named_scope("forward"):
        summed = call(
            forward_kernel, tiles(64), (rows, cols, me, hid, *parts),
            scratch=[pltpu.VMEM((WIDTH_TILES, BLK, BLK), jnp.float32)], flops=8 * macs, moved=6 * 10**6,
        )
    with jax.named_scope("sum_output"):
        output = lax.psum_scatter(summed, "tensor", scatter_dimension=0, tiled=True)
        output = output.transpose(1, 0, 2).reshape(BLK, 4 * BLK)
    with jax.named_scope("backward"):
        wide = jax.ShapeDtypeStruct(gate_pre.shape, jnp.bfloat16)
        d_gate, d_up = call(
            backward_kernel, (wide, wide), (rows, cols, me, grad_tiles, gate_pre, up_pre, *parts),
            scratch=[pltpu.VMEM((HID_TILES, BLK, BLK), jnp.float32)], flops=8 * macs, moved=8 * 10**6,
        )
    with jax.named_scope("sum_terms_second"):
        far_terms = functools.reduce(jnp.add, [a.astype(jnp.float32) for a in far_terms]).astype(jnp.bfloat16)
        far_terms = z_exchange(far_terms)
        near_terms = call(near_sum_kernel, tuple(tiles(1) for _ in range(NX)), (near_terms,), moved=10**6)
        near_terms = [near_terms[0]] + [lax.ppermute(near_terms[s], "fsdp", x_shift(s)) for s in range(1, NX)]
        grad_blocks = call(block_sum_kernel, tiles(OWNED, jnp.float32), (far_terms, *near_terms), moved=10**6)
        grad_blocks = grad_blocks.reshape(OWNED, 1, BLK, BLK)
    return (output, d_gate, d_up, grad_blocks)


def solution(mesh):
    both = P("fsdp", "tensor")
    blocks = P("fsdp", "tensor", None, None)
    index = P(None, "tensor")
    return jax.shard_map(
        shards, mesh=mesh, in_specs=(both, both, both, blocks, index, index),
        out_specs=(both, both, both, blocks), check_vma=False,
    )
```

```python
import functools

import jax
import jax.numpy as jnp
from jax import lax
from jax.experimental import pallas as pl
from jax.experimental.pallas import tpu as pltpu
from jax.sharding import PartitionSpec as P

BLK = 128
HID_TILES = 13
WIDTH_TILES = 64
GROUP_BLOCKS = 96
OWNED = 3
FAR = 2
NX, NY, NZ = 4, 8, 8
STEP = 8
VMEM_BYTES = 48 * 1024 * 1024

SMEM = pl.BlockSpec(memory_space=pltpu.SMEM)
VMEM = pl.BlockSpec(memory_space=pltpu.VMEM)


def x_shift(step):
    return [(z * NX + x, z * NX + (x + step) % NX) for z in range(NZ) for x in range(NX)]


CORE_SWAP = [(t, t ^ 1) for t in range(2 * NY)]
Z_GROUPS = [[z * NX + x for z in range(NZ)] for x in range(NX)]
X_GROUPS = [[z * NX + x for x in range(NX)] for z in range(NZ)]
Y_GROUPS = [[y * 2 + c for y in range(NY)] for c in range(2)]


def call(kernel, outs, ins, scratch=(), flops=0, moved=0):
    return pl.pallas_call(
        kernel,
        out_shape=outs,
        in_specs=[SMEM if a.dtype == jnp.int32 else VMEM for a in ins],
        out_specs=jax.tree.map(lambda _: VMEM, outs),
        scratch_shapes=list(scratch),
        compiler_params=pltpu.CompilerParams(vmem_limit_bytes=VMEM_BYTES),
        cost_estimate=pl.CostEstimate(flops=flops, bytes_accessed=moved, transcendentals=0),
    )(*ins)


def tiles(n, dtype=jnp.bfloat16):
    return jax.ShapeDtypeStruct((n, BLK, BLK), dtype)


def block_of(z, x, place):
    return (z * NX + x) * OWNED + place


def far_at(a, i, me_x, sign):
    return block_of(i // FAR, lax.rem(me_x + sign * a + NX, NX), lax.rem(i, FAR))


def near_at(i, me_x, sign):
    return block_of(i // NX, lax.rem(me_x + sign * lax.rem(i, NX) + NX, NX), FAR)


def each_block(parts, me_x, sign, visit):
    for a, ref in enumerate(parts):
        def some(g, carry, a=a, ref=ref):
            entries = [g * STEP + j for j in range(STEP)]
            visit(ref, [(i, far_at(a, i, me_x, sign) if a < NX else near_at(i, me_x, sign)) for i in entries])
            return carry
        lax.fori_loop(0, ref.shape[0] // STEP, some, 0)


def hidden_kernel(gate_ref, up_ref, hid_ref, hid_t_ref):
    for r in range(HID_TILES):
        here = slice(r * BLK, (r + 1) * BLK)
        gate = gate_ref[:, here].astype(jnp.float32)
        hidden = gate * jax.nn.sigmoid(gate) * up_ref[:, here].astype(jnp.float32)
        hid_ref[r] = hidden.astype(jnp.bfloat16)
        hid_t_ref[r] = hidden.T.astype(jnp.bfloat16)


def terms_kernel(rows_ref, cols_ref, hid_t_ref, grad_ref, out_ref):
    def some(g, carry):
        for j in range(STEP):
            i = g * STEP + j
            z, place = lax.rem(i // OWNED, NZ), lax.rem(i, OWNED)
            k = block_of(z, i // (NZ * OWNED), place)
            out_ref[i] = jnp.dot(
                hid_t_ref[rows_ref[k]], grad_ref[cols_ref[k]], preferred_element_type=jnp.float32
            ).astype(jnp.bfloat16)
        return carry
    lax.fori_loop(0, GROUP_BLOCKS // STEP, some, 0)


def forward_kernel(rows_ref, cols_ref, me_ref, hid_ref, *refs):
    parts, (keep_ref, send_ref, total) = refs[:NX + 1], refs[NX + 1:]
    core = me_ref[1]
    total[...] = jnp.zeros_like(total)

    def visit(ref, entries):
        found = [
            (cols_ref[k], jnp.dot(hid_ref[rows_ref[k]], ref[i], preferred_element_type=jnp.float32)) for i, k in entries
        ]
        for c, value in found:
            total[c] += value
    each_block(parts, me_ref[0], -1, visit)

    def put(y, carry):
        mine, other = (y * 2 + core) * 4, (y * 2 + 1 - core) * 4
        for j in range(4):
            keep_ref[y * 4 + j] = total[mine + j].astype(jnp.bfloat16)
            send_ref[y * 4 + j] = total[other + j].astype(jnp.bfloat16)
        return carry
    lax.fori_loop(0, NY, put, 0)


def backward_kernel(rows_ref, cols_ref, me_ref, grad_ref, gate_ref, up_ref, *refs):
    parts, (d_gate_ref, d_up_ref, total) = refs[:NX + 1], refs[NX + 1:]
    total[...] = jnp.zeros_like(total)

    def visit(ref, entries):
        found = [
            (rows_ref[k], lax.dot_general(
                grad_ref[cols_ref[k]], ref[i], (((1,), (1,)), ((), ())), preferred_element_type=jnp.float32
            )) for i, k in entries
        ]
        for r, value in found:
            total[r] += value
    each_block(parts, me_ref[0], -1, visit)
    for r in range(HID_TILES):
        here = slice(r * BLK, (r + 1) * BLK)
        gate = gate_ref[:, here].astype(jnp.float32)
        up = up_ref[:, here].astype(jnp.float32)
        sigma = jax.nn.sigmoid(gate)
        back = total[r]
        d_gate_ref[:, here] = (back * up * sigma * (1.0 + gate * (1.0 - sigma))).astype(jnp.bfloat16)
        d_up_ref[:, here] = (back * gate * sigma).astype(jnp.bfloat16)


def sum_kernel(parts, arrived_ref, out_ref):
    n = out_ref.shape[0]

    def some(j, carry):
        total = arrived_ref[j].astype(jnp.float32)
        for p in range(1, parts):
            total += arrived_ref[p * n + j].astype(jnp.float32)
        out_ref[j] = total.astype(out_ref.dtype)
        return carry
    lax.fori_loop(0, n, some, 0)


def exchange(a, groups):
    return lax.all_to_all(a, "fsdp", 0, 0, tiled=True, axis_index_groups=groups)


def to_all(a):
    return jnp.broadcast_to(a[None], (NZ, *a.shape)).reshape(NZ * a.shape[0], BLK, BLK)


def shards(gate_pre, up_pre, out_grad, down_blocks, block_rows, block_cols):
    rows, cols = block_rows[:, 0], block_cols[:, 0]
    me = jnp.stack([lax.rem(lax.axis_index("fsdp"), NX), lax.rem(lax.axis_index("tensor"), 2)]).astype(jnp.int32)
    macs = GROUP_BLOCKS * BLK**3
    blocks = down_blocks.reshape(OWNED, BLK, BLK)

    with jax.named_scope("gather_out_grad"):
        grad_tiles = out_grad.reshape(BLK, 4, BLK).transpose(1, 0, 2)
        grad_tiles, blocks = lax.optimization_barrier((grad_tiles, blocks))
        grad_tiles = lax.all_gather(grad_tiles, "tensor", axis=0, tiled=True)
    with jax.named_scope("gather_blocks"):
        far = exchange(to_all(blocks[:FAR]), Z_GROUPS)
        near = blocks[FAR:]
        near = jnp.concatenate([near] + [lax.ppermute(near, "fsdp", x_shift(s)) for s in range(1, NX)], axis=0)
        near = exchange(to_all(near), Z_GROUPS)
        parts = [far] + [lax.ppermute(far, "fsdp", x_shift(s)) for s in range(1, NX)] + [near]
    with jax.named_scope("hidden"):
        hid, hid_t = call(hidden_kernel, (tiles(HID_TILES), tiles(HID_TILES)), (gate_pre, up_pre), flops=10**9, moved=4 * 10**6)
    with jax.named_scope("terms"):
        terms = call(terms_kernel, tiles(GROUP_BLOCKS), (rows, cols, hid_t, grad_tiles), flops=8 * macs, moved=6 * 10**6)
        terms, hid = lax.optimization_barrier((terms, hid))
    with jax.named_scope("sum_terms_x"):
        terms = exchange(terms, X_GROUPS)
    with jax.named_scope("forward"):
        keep, send = call(
            forward_kernel, (tiles(32), tiles(32)), (rows, cols, me, hid, *parts),
            scratch=[pltpu.VMEM((WIDTH_TILES, BLK, BLK), jnp.float32)], flops=8 * macs, moved=6 * 10**6,
        )
    with jax.named_scope("sum_output"):
        swapped = lax.ppermute(send, "tensor", CORE_SWAP)
        pair = (keep.astype(jnp.float32) + swapped.astype(jnp.float32)).astype(jnp.bfloat16)
        pair, me_late = lax.optimization_barrier((pair, me))
        output = lax.psum_scatter(pair, "tensor", scatter_dimension=0, axis_index_groups=Y_GROUPS, tiled=True)
        output = output.transpose(1, 0, 2).reshape(BLK, 4 * BLK)
    with jax.named_scope("backward"):
        wide = jax.ShapeDtypeStruct(gate_pre.shape, jnp.bfloat16)
        d_gate, d_up = call(
            backward_kernel, (wide, wide), (rows, cols, me_late, grad_tiles, gate_pre, up_pre, *parts),
            scratch=[pltpu.VMEM((HID_TILES, BLK, BLK), jnp.float32)], flops=8 * macs, moved=8 * 10**6,
        )
    with jax.named_scope("sum_terms_z"):
        terms, d_gate, d_up = lax.optimization_barrier((terms, d_gate, d_up))
        terms = call(functools.partial(sum_kernel, NX), tiles(NZ * OWNED), (terms,), moved=4 * 10**6)
        terms = exchange(terms, Z_GROUPS)
        grad_blocks = call(functools.partial(sum_kernel, NZ), tiles(OWNED, jnp.float32), (terms,), moved=10**6)
        grad_blocks = grad_blocks.reshape(OWNED, 1, BLK, BLK)
    return (output, d_gate, d_up, grad_blocks)


def solution(mesh):
    both = P("fsdp", "tensor")
    blocks = P("fsdp", "tensor", None, None)
    index = P(None, "tensor")
    return jax.shard_map(
        shards, mesh=mesh, in_specs=(both, both, both, blocks, index, index),
        out_specs=(both, both, both, blocks), check_vma=False,
    )
```

```python
import functools

import jax
import jax.numpy as jnp
from jax import lax
from jax.experimental import pallas as pl
from jax.experimental.pallas import tpu as pltpu
from jax.sharding import PartitionSpec as P

BLK = 128
HID_TILES = 13
WIDTH_TILES = 64
GROUP_BLOCKS = 96
OWNED = 3
FAR = 2
NX, NY, NZ = 4, 8, 8
STEP = 16

SMEM = pl.BlockSpec(memory_space=pltpu.SMEM)
VMEM = pl.BlockSpec(memory_space=pltpu.VMEM)
HBM = pl.BlockSpec(memory_space=pltpu.HBM)


def x_shift(step):
    return [(z * NX + x, z * NX + (x + step) % NX) for z in range(NZ) for x in range(NX)]


CORE_SWAP = [(t, t ^ 1) for t in range(2 * NY)]
Z_GROUPS = [[z * NX + x for z in range(NZ)] for x in range(NX)]
X_GROUPS = [[z * NX + x for x in range(NX)] for z in range(NZ)]
NEAR, APART = 8, 4
NEAR_GROUPS = [[p * NEAR + q for q in range(NEAR)] for p in range(APART)]
APART_GROUPS = [[p * NEAR + q for p in range(APART)] for q in range(NEAR)]
Y_GROUPS = [[y * 2 + c for y in range(NY)] for c in range(2)]


def call(kernel, outs, index, far_ins, near_ins=(), scratch=(), out_spec=VMEM, flops=0, moved=0, vmem=60):
    n, m, k = len(index), len(far_ins), len(near_ins)
    count = len(jax.tree.leaves(outs))

    def body(*refs):
        far = refs[n:n + m]
        rest = refs[n + m:n + m + k + count + len(scratch)]
        buffers, sems = refs[len(refs) - m - 1:-1], refs[-1]
        copies = [pltpu.make_async_copy(src, dst, sems.at[i]) for i, (src, dst) in enumerate(zip(far, buffers))]
        for copy in copies:
            copy.start()

        def fetch(i):
            copies[i].wait()
            return buffers[i]
        kernel(fetch, *refs[:n], *rest)

    return pl.pallas_call(
        body,
        out_shape=outs,
        in_specs=[SMEM] * n + [HBM] * m + [VMEM] * k,
        out_specs=jax.tree.map(lambda _: out_spec, outs),
        scratch_shapes=[*scratch, *[pltpu.VMEM(a.shape, a.dtype) for a in far_ins], pltpu.SemaphoreType.DMA((max(m, 1),))],
        compiler_params=pltpu.CompilerParams(vmem_limit_bytes=vmem * 1024 * 1024),
        cost_estimate=pl.CostEstimate(flops=flops, bytes_accessed=moved, transcendentals=0),
    )(*index, *far_ins, *near_ins)


def tiles(n, dtype=jnp.bfloat16):
    return jax.ShapeDtypeStruct((n, BLK, BLK), dtype)


def block_of(z, x, place):
    return (z * NX + x) * OWNED + place


def far_at(a, i, me_x, sign):
    return block_of(i // FAR, lax.rem(me_x + sign * a + NX, NX), lax.rem(i, FAR))


def near_at(i):
    return block_of(i // NX, lax.rem(i, NX), FAR)


def each_block(fetch, first, me_x, visit):
    for a in range(NX + 1):
        ref = fetch(first + a)

        def some(g, carry, a=a, ref=ref):
            entries = [g * STEP + j for j in range(STEP)]
            visit(ref, [(i, far_at(a, i, me_x, -1) if a < NX else near_at(i)) for i in entries])
            return carry
        lax.fori_loop(0, ref.shape[0] // STEP, some, 0)


def prepare_kernel(fetch, grad_tiles_ref, far_ref, near_ref):
    grad_ref, blocks_ref = fetch(0), fetch(1)
    for t in range(4):
        grad_tiles_ref[t] = grad_ref[:, t * BLK:(t + 1) * BLK]
    for z in range(NZ):
        for j in range(FAR):
            far_ref[z * FAR + j] = blocks_ref[j]
    near_ref[...] = blocks_ref[FAR:]


def hidden_kernel(fetch, hid_ref, hid_t_ref):
    gate_ref, up_ref = fetch(0), fetch(1)
    for r in range(HID_TILES):
        here = slice(r * BLK, (r + 1) * BLK)
        gate = gate_ref[:, here].astype(jnp.float32)
        hidden = gate * jax.nn.sigmoid(gate) * up_ref[:, here].astype(jnp.float32)
        hid_ref[r] = hidden.astype(jnp.bfloat16)
        hid_t_ref[r] = hidden.T.astype(jnp.bfloat16)


def terms_kernel(fetch, rows_ref, cols_ref, out_ref, terms, sems):
    hid_t_ref, grad_ref = fetch(0), fetch(1)

    def leave(g):
        here = pl.ds(g * STEP, STEP)
        return pltpu.make_async_copy(terms.at[here], out_ref.at[here], sems.at[g])

    def some(g, carry):
        for j in range(STEP):
            i = g * STEP + j
            p, q = lax.rem(i // OWNED, APART), i // (APART * OWNED)
            k = (p * NEAR + q) * OWNED + lax.rem(i, OWNED)
            terms[i] = jnp.dot(
                hid_t_ref[rows_ref[k]], grad_ref[cols_ref[k]], preferred_element_type=jnp.float32
            ).astype(jnp.bfloat16)
        leave(g).start()
        return carry
    lax.fori_loop(0, GROUP_BLOCKS // STEP, some, 0)
    for g in range(GROUP_BLOCKS // STEP):
        leave(g).wait()


def forward_kernel(fetch, rows_ref, cols_ref, me_ref, keep_ref, send_ref, total):
    core = me_ref[1]
    total[...] = jnp.zeros_like(total)
    hid_ref = fetch(0)

    def visit(ref, entries):
        found = [
            (cols_ref[k], jnp.dot(hid_ref[rows_ref[k]], ref[i], preferred_element_type=jnp.float32)) for i, k in entries
        ]
        for c, value in found:
            total[c] += value
    each_block(fetch, 1, me_ref[0], visit)

    def put(y, carry):
        mine, other = (y * 2 + core) * 4, (y * 2 + 1 - core) * 4
        for j in range(4):
            keep_ref[y * 4 + j] = total[mine + j].astype(jnp.bfloat16)
            send_ref[y * 4 + j] = total[other + j].astype(jnp.bfloat16)
        return carry
    lax.fori_loop(0, NY, put, 0)


def backward_kernel(fetch, rows_ref, cols_ref, me_ref, d_gate_ref, d_up_ref, total):
    total[...] = jnp.zeros_like(total)
    grad_ref, gate_ref, up_ref = fetch(0), fetch(1), fetch(2)

    def visit(ref, entries):
        found = [
            (rows_ref[k], lax.dot_general(
                grad_ref[cols_ref[k]], ref[i], (((1,), (1,)), ((), ())), preferred_element_type=jnp.float32
            )) for i, k in entries
        ]
        for r, value in found:
            total[r] += value
    each_block(fetch, 3, me_ref[0], visit)
    for r in range(HID_TILES):
        here = slice(r * BLK, (r + 1) * BLK)
        gate = gate_ref[:, here].astype(jnp.float32)
        up = up_ref[:, here].astype(jnp.float32)
        sigma = jax.nn.sigmoid(gate)
        back = total[r]
        d_gate_ref[:, here] = (back * up * sigma * (1.0 + gate * (1.0 - sigma))).astype(jnp.bfloat16)
        d_up_ref[:, here] = (back * gate * sigma).astype(jnp.bfloat16)


def pair_kernel(fetch, keep_ref, swapped_ref, out_ref, pair, sems):
    def leave(g):
        here = pl.ds(g * 8, 8)
        return pltpu.make_async_copy(pair.at[here], out_ref.at[here], sems.at[g])

    for g in range(4):
        here = pl.ds(g * 8, 8)
        pair[here] = (keep_ref[here].astype(jnp.float32) + swapped_ref[here].astype(jnp.float32)).astype(jnp.bfloat16)
        leave(g).start()
    for g in range(4):
        leave(g).wait()


def output_kernel(fetch, out_ref):
    tiles_ref = fetch(0)
    for t in range(4):
        out_ref[:, t * BLK:(t + 1) * BLK] = tiles_ref[t]


def sum_kernel(parts, fetch, arrived_ref, out_ref):
    n = out_ref.shape[0]
    for j in range(n):
        total = arrived_ref[j].astype(jnp.float32)
        for p in range(1, parts):
            total += arrived_ref[p * n + j].astype(jnp.float32)
        out_ref[j] = total.astype(out_ref.dtype)


def exchange(a, groups):
    return lax.all_to_all(a, "fsdp", 0, 0, tiled=True, axis_index_groups=groups)


def to_all(a):
    return jnp.broadcast_to(a[None], (NZ, *a.shape)).reshape(NZ * a.shape[0], BLK, BLK)


def shards(gate_pre, up_pre, out_grad, down_blocks, block_rows, block_cols):
    rows, cols = block_rows[:, 0], block_cols[:, 0]
    me = jnp.stack([lax.rem(lax.axis_index("fsdp"), NX), lax.rem(lax.axis_index("tensor"), 2)]).astype(jnp.int32)
    macs = GROUP_BLOCKS * BLK**3
    blocks = down_blocks.reshape(OWNED, BLK, BLK)

    with jax.named_scope("gather_out_grad"):
        grad_tiles, far, near = call(
            prepare_kernel, (tiles(4), tiles(NZ * FAR), tiles(OWNED - FAR)), (), (out_grad, blocks), moved=10**6
        )
        grad_tiles = lax.all_gather(grad_tiles, "tensor", axis=0, tiled=True)
    with jax.named_scope("gather_blocks"):
        far = exchange(far, Z_GROUPS)
        near = lax.all_gather(near, "fsdp", axis=0, axis_index_groups=X_GROUPS, tiled=True)
        near = exchange(to_all(near), Z_GROUPS)
        parts = [far] + [lax.ppermute(far, "fsdp", x_shift(s)) for s in range(1, NX)] + [near]
    with jax.named_scope("hidden"):
        hid, hid_t = call(hidden_kernel, (tiles(HID_TILES), tiles(HID_TILES)), (), (gate_pre, up_pre), flops=10**9, moved=4 * 10**6)
    with jax.named_scope("terms"):
        terms = call(
            terms_kernel, tiles(GROUP_BLOCKS), (rows, cols), (hid_t, grad_tiles), out_spec=HBM,
            scratch=[pltpu.VMEM((GROUP_BLOCKS, BLK, BLK), jnp.bfloat16), pltpu.SemaphoreType.DMA((GROUP_BLOCKS // STEP,))],
            flops=8 * macs, moved=6 * 10**6,
        )
        terms, hid = lax.optimization_barrier((terms, hid))
    with jax.named_scope("sum_terms_near"):
        terms, parts = lax.optimization_barrier((terms, parts))
        terms = exchange(terms, NEAR_GROUPS)
    with jax.named_scope("forward"):
        keep, send = call(
            forward_kernel, (tiles(32), tiles(32)), (rows, cols, me), (hid, *parts),
            scratch=[pltpu.VMEM((WIDTH_TILES, BLK, BLK), jnp.float32)], flops=8 * macs, moved=6 * 10**6, vmem=60,
        )
    with jax.named_scope("sum_output"):
        swapped = lax.ppermute(send, "tensor", CORE_SWAP)
        pair = call(
            pair_kernel, tiles(32), (), (), (keep, swapped), out_spec=HBM,
            scratch=[pltpu.VMEM((32, BLK, BLK), jnp.bfloat16), pltpu.SemaphoreType.DMA((4,))], moved=3 * 10**6, vmem=60,
        )
        pair, me_late = lax.optimization_barrier((pair, me))
        output = lax.psum_scatter(pair, "tensor", scatter_dimension=0, axis_index_groups=Y_GROUPS, tiled=True)
        output = call(output_kernel, jax.ShapeDtypeStruct(out_grad.shape, jnp.bfloat16), (), (output,), moved=10**5)
    with jax.named_scope("backward"):
        wide = jax.ShapeDtypeStruct(gate_pre.shape, jnp.bfloat16)
        d_gate, d_up = call(
            backward_kernel, (wide, wide), (rows, cols, me_late), (grad_tiles, gate_pre, up_pre, *parts),
            scratch=[pltpu.VMEM((HID_TILES, BLK, BLK), jnp.float32)], flops=8 * macs, moved=8 * 10**6, vmem=60,
        )
    with jax.named_scope("sum_terms_apart"):
        terms, d_gate, d_up = lax.optimization_barrier((terms, d_gate, d_up))
        terms = call(functools.partial(sum_kernel, NEAR), tiles(APART * OWNED), (), (), (terms,), moved=4 * 10**6, vmem=24)
        terms = exchange(terms, APART_GROUPS)
        grad_blocks = call(functools.partial(sum_kernel, APART), tiles(OWNED, jnp.float32), (), (), (terms,), moved=10**6, vmem=24)
        grad_blocks = grad_blocks.reshape(OWNED, 1, BLK, BLK)
    return (output, d_gate, d_up, grad_blocks)


def solution(mesh):
    both = P("fsdp", "tensor")
    blocks = P("fsdp", "tensor", None, None)
    index = P(None, "tensor")
    return jax.shard_map(
        shards, mesh=mesh, in_specs=(both, both, both, blocks, index, index),
        out_specs=(both, both, both, blocks), check_vma=False,
    )
```

```python
import functools

import jax
import jax.numpy as jnp
from jax import lax
from jax.experimental import pallas as pl
from jax.experimental.pallas import tpu as pltpu
from jax.sharding import PartitionSpec as P

BLK = 128
HID_TILES = 13
WIDTH_TILES = 64
GROUP_BLOCKS = 96
OWNED = 3
FAR = 2
NX, NY, NZ = 4, 8, 8
STEP = 16

SMEM = pl.BlockSpec(memory_space=pltpu.SMEM)
VMEM = pl.BlockSpec(memory_space=pltpu.VMEM)
HBM = pl.BlockSpec(memory_space=pltpu.HBM)


def x_shift(step):
    return [(z * NX + x, z * NX + (x + step) % NX) for z in range(NZ) for x in range(NX)]


CORE_SWAP = [(t, t ^ 1) for t in range(2 * NY)]
Z_GROUPS = [[z * NX + x for z in range(NZ)] for x in range(NX)]
X_GROUPS = [[z * NX + x for x in range(NX)] for z in range(NZ)]
NEAR, APART = 8, 4
NEAR_GROUPS = [[p * NEAR + q for q in range(NEAR)] for p in range(APART)]
APART_GROUPS = [[p * NEAR + q for p in range(APART)] for q in range(NEAR)]
Y_GROUPS = [[y * 2 + c for y in range(NY)] for c in range(2)]


def call(kernel, outs, index, far_ins, near_ins=(), scratch=(), out_spec=VMEM, near_spec=VMEM, flops=0, moved=0, vmem=60):
    n, m, k = len(index), len(far_ins), len(near_ins)
    count = len(jax.tree.leaves(outs))

    def body(*refs):
        far = refs[n:n + m]
        rest = refs[n + m:n + m + k + count + len(scratch)]
        buffers, sems = refs[len(refs) - m - 1:-1], refs[-1]
        copies = [pltpu.make_async_copy(src, dst, sems.at[i]) for i, (src, dst) in enumerate(zip(far, buffers))]
        for copy in copies:
            copy.start()

        def fetch(i):
            copies[i].wait()
            return buffers[i]
        kernel(fetch, *refs[:n], *rest)

    return pl.pallas_call(
        body,
        out_shape=outs,
        in_specs=[SMEM] * n + [HBM] * m + [near_spec] * k,
        out_specs=jax.tree.map(lambda _: out_spec, outs),
        scratch_shapes=[*scratch, *[pltpu.VMEM(a.shape, a.dtype) for a in far_ins], pltpu.SemaphoreType.DMA((max(m, 1),))],
        compiler_params=pltpu.CompilerParams(vmem_limit_bytes=vmem * 1024 * 1024),
        cost_estimate=pl.CostEstimate(flops=flops, bytes_accessed=moved, transcendentals=0),
    )(*index, *far_ins, *near_ins)


def tiles(n, dtype=jnp.bfloat16):
    return jax.ShapeDtypeStruct((n, BLK, BLK), dtype)


def block_of(z, x, place):
    return (z * NX + x) * OWNED + place


def far_at(a, i, me_x, sign):
    return block_of(i // FAR, lax.rem(me_x + sign * a + NX, NX), lax.rem(i, FAR))


def near_at(i):
    return block_of(i // NX, lax.rem(i, NX), FAR)


def each_block(fetch, first, me_x, visit):
    for a in range(NX + 1):
        ref = fetch(first + a)

        def some(g, carry, a=a, ref=ref):
            entries = [g * STEP + j for j in range(STEP)]
            visit(ref, [(i, far_at(a, i, me_x, -1) if a < NX else near_at(i)) for i in entries])
            return carry
        lax.fori_loop(0, ref.shape[0] // STEP, some, 0)


def prepare_kernel(fetch, grad_tiles_ref, far_ref, near_ref):
    grad_ref, blocks_ref = fetch(0), fetch(1)
    for t in range(4):
        grad_tiles_ref[t] = grad_ref[:, t * BLK:(t + 1) * BLK]
    for z in range(NZ):
        for j in range(FAR):
            far_ref[z * FAR + j] = blocks_ref[j]
    near_ref[...] = blocks_ref[FAR:]


def hidden_kernel(fetch, hid_ref, hid_t_ref):
    gate_ref, up_ref = fetch(0), fetch(1)
    for r in range(HID_TILES):
        here = slice(r * BLK, (r + 1) * BLK)
        gate = gate_ref[:, here].astype(jnp.float32)
        hidden = gate * jax.nn.sigmoid(gate) * up_ref[:, here].astype(jnp.float32)
        hid_ref[r] = hidden.astype(jnp.bfloat16)
        hid_t_ref[r] = hidden.T.astype(jnp.bfloat16)


def terms_kernel(fetch, rows_ref, cols_ref, out_ref, terms, sems):
    hid_t_ref, grad_ref = fetch(0), fetch(1)

    def leave(g):
        here = pl.ds(g * STEP, STEP)
        return pltpu.make_async_copy(terms.at[here], out_ref.at[here], sems.at[g])

    def some(g, carry):
        for j in range(STEP):
            i = g * STEP + j
            p, q = lax.rem(i // OWNED, APART), i // (APART * OWNED)
            k = (p * NEAR + q) * OWNED + lax.rem(i, OWNED)
            terms[i] = jnp.dot(
                hid_t_ref[rows_ref[k]], grad_ref[cols_ref[k]], preferred_element_type=jnp.float32
            ).astype(jnp.bfloat16)
        leave(g).start()
        return carry
    lax.fori_loop(0, GROUP_BLOCKS // STEP, some, 0)
    for g in range(GROUP_BLOCKS // STEP):
        leave(g).wait()


def forward_kernel(fetch, rows_ref, cols_ref, keep_ref, send_ref, total, keep, send, sems):
    me_x, core = lax.rem(lax.axis_index("fsdp"), NX), lax.rem(lax.axis_index("tensor"), 2)
    total[...] = jnp.zeros_like(total)
    hid_ref = fetch(0)

    def visit(ref, entries):
        found = [
            (cols_ref[k], jnp.dot(hid_ref[rows_ref[k]], ref[i], preferred_element_type=jnp.float32)) for i, k in entries
        ]
        for c, value in found:
            total[c] += value
    each_block(fetch, 1, me_x, visit)

    def leave(y):
        here = pl.ds(y * 4, 4)
        return [
            pltpu.make_async_copy(src.at[here], dst.at[here], sems.at[i, y])
            for i, (src, dst) in enumerate(((send, send_ref), (keep, keep_ref)))
        ]

    def put(y, carry):
        mine, other = (y * 2 + core) * 4, (y * 2 + 1 - core) * 4
        here = pl.ds(y * 4, 4)
        send[here] = total[pl.ds(other, 4)].astype(jnp.bfloat16)
        keep[here] = total[pl.ds(mine, 4)].astype(jnp.bfloat16)
        for copy in leave(y):
            copy.start()
        return carry
    lax.fori_loop(0, NY, put, 0)
    for y in range(NY):
        for copy in leave(y):
            copy.wait()


def backward_kernel(fetch, rows_ref, cols_ref, d_gate_ref, d_up_ref, total):
    total[...] = jnp.zeros_like(total)
    grad_ref, gate_ref, up_ref = fetch(0), fetch(1), fetch(2)

    def visit(ref, entries):
        found = [
            (rows_ref[k], lax.dot_general(
                grad_ref[cols_ref[k]], ref[i], (((1,), (1,)), ((), ())), preferred_element_type=jnp.float32
            )) for i, k in entries
        ]
        for r, value in found:
            total[r] += value
    each_block(fetch, 3, lax.rem(lax.axis_index("fsdp"), NX), visit)
    for r in range(HID_TILES):
        here = slice(r * BLK, (r + 1) * BLK)
        gate = gate_ref[:, here].astype(jnp.float32)
        up = up_ref[:, here].astype(jnp.float32)
        sigma = jax.nn.sigmoid(gate)
        back = total[r]
        d_gate_ref[:, here] = (back * up * sigma * (1.0 + gate * (1.0 - sigma))).astype(jnp.bfloat16)
        d_up_ref[:, here] = (back * gate * sigma).astype(jnp.bfloat16)


def pair_kernel(fetch, keep_ref, swapped_ref, out_ref, keep, swapped, pair, sems):
    parts = [pl.ds(g * 8, 8) for g in range(4)]
    arrive = [
        [pltpu.make_async_copy(src.at[here], dst.at[here], sems.at[i, g]) for i, (src, dst) in enumerate(((keep_ref, keep), (swapped_ref, swapped)))]
        for g, here in enumerate(parts)
    ]
    leave = [pltpu.make_async_copy(pair.at[here], out_ref.at[here], sems.at[2, g]) for g, here in enumerate(parts)]
    for copies in arrive:
        for copy in copies:
            copy.start()
    for g, here in enumerate(parts):
        for copy in arrive[g]:
            copy.wait()
        pair[here] = (keep[here].astype(jnp.float32) + swapped[here].astype(jnp.float32)).astype(jnp.bfloat16)
        leave[g].start()
    for copy in leave:
        copy.wait()


def output_kernel(fetch, out_ref):
    tiles_ref = fetch(0)
    for t in range(4):
        out_ref[:, t * BLK:(t + 1) * BLK] = tiles_ref[t]


def sum_kernel(parts, fetch, arrived_ref, out_ref):
    n = out_ref.shape[0]
    for j in range(n):
        total = arrived_ref[j].astype(jnp.float32)
        for p in range(1, parts):
            total += arrived_ref[p * n + j].astype(jnp.float32)
        out_ref[j] = total.astype(out_ref.dtype)


def exchange(a, groups):
    return lax.all_to_all(a, "fsdp", 0, 0, tiled=True, axis_index_groups=groups)


def to_all(a):
    return jnp.broadcast_to(a[None], (NZ, *a.shape)).reshape(NZ * a.shape[0], BLK, BLK)


def shards(gate_pre, up_pre, out_grad, down_blocks, block_rows, block_cols):
    rows, cols = block_rows[:, 0], block_cols[:, 0]
    macs = GROUP_BLOCKS * BLK**3
    blocks = down_blocks.reshape(OWNED, BLK, BLK)

    with jax.named_scope("gather_out_grad"):
        grad_tiles, far, near = call(
            prepare_kernel, (tiles(4), tiles(NZ * FAR), tiles(OWNED - FAR)), (), (out_grad, blocks), moved=10**6
        )
        grad_tiles = lax.all_gather(grad_tiles, "tensor", axis=0, tiled=True)
    with jax.named_scope("gather_blocks"):
        far = exchange(far, Z_GROUPS)
        near = lax.all_gather(near, "fsdp", axis=0, axis_index_groups=X_GROUPS, tiled=True)
        near = exchange(to_all(near), Z_GROUPS)
        parts = [far] + [lax.ppermute(far, "fsdp", x_shift(s)) for s in range(1, NX)] + [near]
    with jax.named_scope("hidden"):
        hid, hid_t = call(hidden_kernel, (tiles(HID_TILES), tiles(HID_TILES)), (), (gate_pre, up_pre), flops=10**9, moved=4 * 10**6)
    with jax.named_scope("terms"):
        terms = call(
            terms_kernel, tiles(GROUP_BLOCKS), (rows, cols), (hid_t, grad_tiles), out_spec=HBM,
            scratch=[pltpu.VMEM((GROUP_BLOCKS, BLK, BLK), jnp.bfloat16), pltpu.SemaphoreType.DMA((GROUP_BLOCKS // STEP,))],
            flops=8 * macs, moved=6 * 10**6,
        )
        terms, hid = lax.optimization_barrier((terms, hid))
    with jax.named_scope("sum_terms_near"):
        terms = exchange(terms, NEAR_GROUPS)
    with jax.named_scope("forward"):
        keep, send = call(
            forward_kernel, (tiles(32), tiles(32)), (rows, cols), (hid, *parts), out_spec=HBM,
            scratch=[
                pltpu.VMEM((WIDTH_TILES, BLK, BLK), jnp.float32), pltpu.VMEM((32, BLK, BLK), jnp.bfloat16),
                pltpu.VMEM((32, BLK, BLK), jnp.bfloat16), pltpu.SemaphoreType.DMA((2, NY)),
            ],
            flops=200 * macs, moved=6 * 10**6,
        )
    with jax.named_scope("sum_output"):
        swapped = lax.ppermute(send, "tensor", CORE_SWAP)
        pair = call(
            pair_kernel, tiles(32), (), (), (keep, swapped), out_spec=HBM, near_spec=HBM,
            scratch=[*[pltpu.VMEM((32, BLK, BLK), jnp.bfloat16)] * 3, pltpu.SemaphoreType.DMA((3, 4))], moved=3 * 10**6,
        )
        pair, rows_late = lax.optimization_barrier((pair, rows))
        output = lax.psum_scatter(pair, "tensor", scatter_dimension=0, axis_index_groups=Y_GROUPS, tiled=True)
        output = call(output_kernel, jax.ShapeDtypeStruct(out_grad.shape, jnp.bfloat16), (), (output,), moved=10**5)
    with jax.named_scope("backward"):
        wide = jax.ShapeDtypeStruct(gate_pre.shape, jnp.bfloat16)
        d_gate, d_up = call(
            backward_kernel, (wide, wide), (rows_late, cols), (grad_tiles, gate_pre, up_pre, *parts),
            scratch=[pltpu.VMEM((HID_TILES, BLK, BLK), jnp.float32)], flops=8 * macs, moved=8 * 10**6, vmem=60,
        )
    with jax.named_scope("sum_terms_apart"):
        terms, d_gate, d_up = lax.optimization_barrier((terms, d_gate, d_up))
        terms = call(functools.partial(sum_kernel, NEAR), tiles(APART * OWNED), (), (), (terms,), moved=4 * 10**6, vmem=24)
        terms = exchange(terms, APART_GROUPS)
        grad_blocks = call(functools.partial(sum_kernel, APART), tiles(OWNED, jnp.float32), (), (), (terms,), moved=10**6, vmem=24)
        grad_blocks = grad_blocks.reshape(OWNED, 1, BLK, BLK)
    return (output, d_gate, d_up, grad_blocks)


def solution(mesh):
    both = P("fsdp", "tensor")
    blocks = P("fsdp", "tensor", None, None)
    index = P(None, "tensor")
    return jax.shard_map(
        shards, mesh=mesh, in_specs=(both, both, both, blocks, index, index),
        out_specs=(both, both, both, blocks), check_vma=False,
    )
```

```python
import functools

import jax
import jax.numpy as jnp
from jax import lax
from jax.experimental import pallas as pl
from jax.experimental.pallas import tpu as pltpu
from jax.sharding import PartitionSpec as P

BLK = 128
HID_TILES = 13
WIDTH_TILES = 64
GROUP_BLOCKS = 96
OWNED = 3
FAR = 2
NX, NY, NZ = 4, 8, 8
STEP = 16

SMEM = pl.BlockSpec(memory_space=pltpu.SMEM)
VMEM = pl.BlockSpec(memory_space=pltpu.VMEM)
HBM = pl.BlockSpec(memory_space=pltpu.HBM)


def x_shift(step):
    return [(z * NX + x, z * NX + (x + step) % NX) for z in range(NZ) for x in range(NX)]


CORE_SWAP = [(t, t ^ 1) for t in range(2 * NY)]
Z_GROUPS = [[z * NX + x for z in range(NZ)] for x in range(NX)]
X_GROUPS = [[z * NX + x for x in range(NX)] for z in range(NZ)]
NEAR, APART = 8, 4
NEAR_GROUPS = [[p * NEAR + q for q in range(NEAR)] for p in range(APART)]
APART_GROUPS = [[p * NEAR + q for p in range(APART)] for q in range(NEAR)]
Y_GROUPS = [[y * 2 + c for y in range(NY)] for c in range(2)]


def call(kernel, outs, index, far_ins, near_ins=(), scratch=(), out_spec=VMEM, near_spec=VMEM, flops=0, moved=0, vmem=60):
    n, m, k = len(index), len(far_ins), len(near_ins)
    count = len(jax.tree.leaves(outs))

    def body(*refs):
        far = refs[n:n + m]
        rest = refs[n + m:n + m + k + count + len(scratch)]
        buffers, sems = refs[len(refs) - m - 1:-1], refs[-1]
        copies = [pltpu.make_async_copy(src, dst, sems.at[i]) for i, (src, dst) in enumerate(zip(far, buffers))]
        for copy in copies:
            copy.start()

        def fetch(i):
            copies[i].wait()
            return buffers[i]
        kernel(fetch, *refs[:n], *rest)

    return pl.pallas_call(
        body,
        out_shape=outs,
        in_specs=[SMEM] * n + [HBM] * m + [near_spec] * k,
        out_specs=jax.tree.map(lambda _: out_spec, outs),
        scratch_shapes=[*scratch, *[pltpu.VMEM(a.shape, a.dtype) for a in far_ins], pltpu.SemaphoreType.DMA((max(m, 1),))],
        compiler_params=pltpu.CompilerParams(vmem_limit_bytes=vmem * 1024 * 1024),
        cost_estimate=pl.CostEstimate(flops=flops, bytes_accessed=moved, transcendentals=0),
    )(*index, *far_ins, *near_ins)


def tiles(n, dtype=jnp.bfloat16):
    return jax.ShapeDtypeStruct((n, BLK, BLK), dtype)


def block_of(z, x, place):
    return (z * NX + x) * OWNED + place


def far_at(a, i, me_x, sign):
    return block_of(i // FAR, lax.rem(me_x + sign * a + NX, NX), lax.rem(i, FAR))


def near_at(i):
    return block_of(i // NX, lax.rem(i, NX), FAR)


def each_block(fetch, first, near_ref, me_x, visit):
    for a in range(NX + 1):
        ref = fetch(first + a) if a < NX else near_ref

        def some(g, carry, a=a, ref=ref):
            entries = [g * STEP + j for j in range(STEP)]
            visit(ref, [(i, far_at(a, i, me_x, -1) if a < NX else near_at(i)) for i in entries])
            return carry
        lax.fori_loop(0, ref.shape[0] // STEP, some, 0)


def prepare_kernel(fetch, grad_tiles_ref, far_ref, near_ref):
    grad_ref, blocks_ref = fetch(0), fetch(1)
    for t in range(4):
        grad_tiles_ref[t] = grad_ref[:, t * BLK:(t + 1) * BLK]
    for z in range(NZ):
        for j in range(FAR):
            far_ref[z * FAR + j] = blocks_ref[j]
    near_ref[...] = blocks_ref[FAR:]


def hidden_kernel(fetch, hid_ref, hid_t_ref):
    gate_ref, up_ref = fetch(0), fetch(1)
    for r in range(HID_TILES):
        here = slice(r * BLK, (r + 1) * BLK)
        gate = gate_ref[:, here].astype(jnp.float32)
        hidden = gate * jax.nn.sigmoid(gate) * up_ref[:, here].astype(jnp.float32)
        hid_ref[r] = hidden.astype(jnp.bfloat16)
        hid_t_ref[r] = hidden.T.astype(jnp.bfloat16)


def terms_kernel(fetch, rows_ref, cols_ref, out_ref, terms, sems):
    hid_t_ref, grad_ref = fetch(0), fetch(1)

    def leave(g):
        here = pl.ds(g * STEP, STEP)
        return pltpu.make_async_copy(terms.at[here], out_ref.at[here], sems.at[g])

    def some(g, carry):
        for j in range(STEP):
            i = g * STEP + j
            p, q = lax.rem(i // OWNED, APART), i // (APART * OWNED)
            k = (p * NEAR + q) * OWNED + lax.rem(i, OWNED)
            terms[i] = jnp.dot(
                hid_t_ref[rows_ref[k]], grad_ref[cols_ref[k]], preferred_element_type=jnp.float32
            ).astype(jnp.bfloat16)
        leave(g).start()
        return carry
    lax.fori_loop(0, GROUP_BLOCKS // STEP, some, 0)
    for g in range(GROUP_BLOCKS // STEP):
        leave(g).wait()


def forward_kernel(fetch, rows_ref, cols_ref, near_ref, keep_ref, send_ref, total, keep, send, sems):
    me_x, core = lax.rem(lax.axis_index("fsdp"), NX), lax.rem(lax.axis_index("tensor"), 2)
    total[...] = jnp.zeros_like(total)
    hid_ref = fetch(0)

    def visit(ref, entries):
        found = [
            (cols_ref[k], jnp.dot(hid_ref[rows_ref[k]], ref[i], preferred_element_type=jnp.float32)) for i, k in entries
        ]
        for c, value in found:
            total[c] += value
    each_block(fetch, 1, near_ref, me_x, visit)

    def leave(y):
        here = pl.ds(y * 4, 4)
        return [
            pltpu.make_async_copy(src.at[here], dst.at[here], sems.at[i, y])
            for i, (src, dst) in enumerate(((send, send_ref), (keep, keep_ref)))
        ]

    def put(y, carry):
        mine, other = (y * 2 + core) * 4, (y * 2 + 1 - core) * 4
        here = pl.ds(y * 4, 4)
        send[here] = total[pl.ds(other, 4)].astype(jnp.bfloat16)
        keep[here] = total[pl.ds(mine, 4)].astype(jnp.bfloat16)
        for copy in leave(y):
            copy.start()
        return carry
    lax.fori_loop(0, NY, put, 0)
    for y in range(NY):
        for copy in leave(y):
            copy.wait()


def backward_kernel(fetch, rows_ref, cols_ref, near_ref, d_gate_ref, d_up_ref, total):
    total[...] = jnp.zeros_like(total)
    grad_ref, gate_ref, up_ref = fetch(0), fetch(1), fetch(2)

    def visit(ref, entries):
        found = [
            (rows_ref[k], lax.dot_general(
                grad_ref[cols_ref[k]], ref[i], (((1,), (1,)), ((), ())), preferred_element_type=jnp.float32
            )) for i, k in entries
        ]
        for r, value in found:
            total[r] += value
    each_block(fetch, 3, near_ref, lax.rem(lax.axis_index("fsdp"), NX), visit)
    for r in range(HID_TILES):
        here = slice(r * BLK, (r + 1) * BLK)
        gate = gate_ref[:, here].astype(jnp.float32)
        up = up_ref[:, here].astype(jnp.float32)
        sigma = jax.nn.sigmoid(gate)
        back = total[r]
        d_gate_ref[:, here] = (back * up * sigma * (1.0 + gate * (1.0 - sigma))).astype(jnp.bfloat16)
        d_up_ref[:, here] = (back * gate * sigma).astype(jnp.bfloat16)


def pair_kernel(fetch, keep_ref, swapped_ref, out_ref, keep, swapped, pair, sems):
    parts = [pl.ds(g * 8, 8) for g in range(4)]
    arrive = [
        [pltpu.make_async_copy(src.at[here], dst.at[here], sems.at[i, g]) for i, (src, dst) in enumerate(((keep_ref, keep), (swapped_ref, swapped)))]
        for g, here in enumerate(parts)
    ]
    leave = [pltpu.make_async_copy(pair.at[here], out_ref.at[here], sems.at[2, g]) for g, here in enumerate(parts)]
    for copies in arrive:
        for copy in copies:
            copy.start()
    for g, here in enumerate(parts):
        for copy in arrive[g]:
            copy.wait()
        pair[here] = (keep[here].astype(jnp.float32) + swapped[here].astype(jnp.float32)).astype(jnp.bfloat16)
        leave[g].start()
    for copy in leave:
        copy.wait()


def output_kernel(fetch, out_ref):
    tiles_ref = fetch(0)
    for t in range(4):
        out_ref[:, t * BLK:(t + 1) * BLK] = tiles_ref[t]


def sum_kernel(parts, fetch, arrived_ref, out_ref):
    n = out_ref.shape[0]
    for j in range(n):
        total = arrived_ref[j].astype(jnp.float32)
        for p in range(1, parts):
            total += arrived_ref[p * n + j].astype(jnp.float32)
        out_ref[j] = total.astype(out_ref.dtype)


def exchange(a, groups):
    return lax.all_to_all(a, "fsdp", 0, 0, tiled=True, axis_index_groups=groups)


def to_all(a):
    return jnp.broadcast_to(a[None], (NZ, *a.shape)).reshape(NZ * a.shape[0], BLK, BLK)


def shards(gate_pre, up_pre, out_grad, down_blocks, block_rows, block_cols):
    rows, cols = block_rows[:, 0], block_cols[:, 0]
    macs = GROUP_BLOCKS * BLK**3
    blocks = down_blocks.reshape(OWNED, BLK, BLK)

    with jax.named_scope("gather_out_grad"):
        grad_tiles, far, near = call(
            prepare_kernel, (tiles(4), tiles(NZ * FAR), tiles(OWNED - FAR)), (), (out_grad, blocks), moved=10**6
        )
        grad_tiles = lax.all_gather(grad_tiles, "tensor", axis=0, tiled=True)
    with jax.named_scope("gather_blocks"):
        far = exchange(far, Z_GROUPS)
        near = lax.all_gather(near, "fsdp", axis=0, axis_index_groups=X_GROUPS, tiled=True)
        near = exchange(to_all(near), Z_GROUPS)
        parts = [far] + [lax.ppermute(far, "fsdp", x_shift(s)) for s in range(1, NX)] + [near]
    with jax.named_scope("hidden"):
        hid, hid_t = call(hidden_kernel, (tiles(HID_TILES), tiles(HID_TILES)), (), (gate_pre, up_pre), flops=10**9, moved=4 * 10**6)
    with jax.named_scope("terms"):
        terms = call(
            terms_kernel, tiles(GROUP_BLOCKS), (rows, cols), (hid_t, grad_tiles), out_spec=HBM,
            scratch=[pltpu.VMEM((GROUP_BLOCKS, BLK, BLK), jnp.bfloat16), pltpu.SemaphoreType.DMA((GROUP_BLOCKS // STEP,))],
            flops=8 * macs, moved=6 * 10**6,
        )
        terms, hid = lax.optimization_barrier((terms, hid))
    with jax.named_scope("sum_terms_near"):
        terms = exchange(terms, NEAR_GROUPS)
    with jax.named_scope("forward"):
        keep, send = call(
            forward_kernel, (tiles(32), tiles(32)), (rows, cols), (hid, *parts[:NX]), (parts[NX],), out_spec=HBM, vmem=56,
            scratch=[
                pltpu.VMEM((WIDTH_TILES, BLK, BLK), jnp.float32), pltpu.VMEM((32, BLK, BLK), jnp.bfloat16),
                pltpu.VMEM((32, BLK, BLK), jnp.bfloat16), pltpu.SemaphoreType.DMA((2, NY)),
            ],
            flops=200 * macs, moved=6 * 10**6,
        )
    with jax.named_scope("sum_output"):
        swapped = lax.ppermute(send, "tensor", CORE_SWAP)
        pair = call(
            pair_kernel, tiles(32), (), (), (keep, swapped), out_spec=HBM, near_spec=HBM,
            scratch=[*[pltpu.VMEM((32, BLK, BLK), jnp.bfloat16)] * 3, pltpu.SemaphoreType.DMA((3, 4))], moved=3 * 10**6, vmem=56,
        )
        pair, rows_late = lax.optimization_barrier((pair, rows))
        output = lax.psum_scatter(pair, "tensor", scatter_dimension=0, axis_index_groups=Y_GROUPS, tiled=True)
        output = call(output_kernel, jax.ShapeDtypeStruct(out_grad.shape, jnp.bfloat16), (), (output,), moved=10**5)
    with jax.named_scope("backward"):
        wide = jax.ShapeDtypeStruct(gate_pre.shape, jnp.bfloat16)
        d_gate, d_up = call(
            backward_kernel, (wide, wide), (rows_late, cols), (grad_tiles, gate_pre, up_pre, *parts[:NX]), (parts[NX],),
            scratch=[pltpu.VMEM((HID_TILES, BLK, BLK), jnp.float32)], flops=8 * macs, moved=8 * 10**6, vmem=56,
        )
    with jax.named_scope("sum_terms_apart"):
        terms, d_gate, d_up = lax.optimization_barrier((terms, d_gate, d_up))
        terms = call(functools.partial(sum_kernel, NEAR), tiles(APART * OWNED), (), (), (terms,), moved=4 * 10**6, vmem=24)
        terms = exchange(terms, APART_GROUPS)
        grad_blocks = call(functools.partial(sum_kernel, APART), tiles(OWNED, jnp.float32), (), (), (terms,), moved=10**6, vmem=24)
        grad_blocks = grad_blocks.reshape(OWNED, 1, BLK, BLK)
    return (output, d_gate, d_up, grad_blocks)


def solution(mesh):
    both = P("fsdp", "tensor")
    blocks = P("fsdp", "tensor", None, None)
    index = P(None, "tensor")
    return jax.shard_map(
        shards, mesh=mesh, in_specs=(both, both, both, blocks, index, index),
        out_specs=(both, both, both, blocks), check_vma=False,
    )
```
